256 devices in a mesh: lat: 32 (over z, y), lon: 8 (over x, core).
Axes of the slice: x: 4, y: 4, z: 8, core: 2. Of those that a mesh axis runs over, the one named last changes fastest.
Arguments:
- fields: bfloat16 [2, 256, 512, 768], P(None, 'lat', 'lon'), may hold values from -6 to 6
- cotangent: bfloat16 [2, 256, 512, 768], P(None, 'lat', 'lon'), may hold values from -6 to 6
- kept_mask: int32 [128, 128, 8], P(None, 'lat', 'lon'), may hold values 0 or 1
- w_one: bfloat16 [8, 2, 96, 96], P('lon'), may hold values from -0.4375 to 0.4375
- b_one: bfloat16 [8, 2, 96], P('lon'), may hold values from -3 to 3
- w_two: bfloat16 [8, 2, 96, 96], P('lon'), may hold values from -0.4375 to 0.4375
- b_two: bfloat16 [8, 2, 96], P('lon'), may hold values from -3 to 3
Outputs:
- mixed: bfloat16 [2, 256, 512, 768], P(None, 'lat', 'lon')
- grad_fields: bfloat16 [2, 256, 512, 768], P(None, 'lat', 'lon')
- grad_w_one: float32 [8, 2, 96, 96], P('lon')
- grad_b_one: float32 [8, 2, 96], P('lon')
- grad_w_two: float32 [8, 2, 96, 96], P('lon')
- grad_b_two: float32 [8, 2, 96], P('lon')
The draws below stay inside these ranges and needn't reach their ends.
All inputs are finite; a program needn't handle non-finite values. No bound on the sum of `kept_mask` on one device may be relied on, other than what follows from the above.
Results may differ from the reference program's by a relative error of at most 0.023.
Values may be sent and summed in bfloat16 or wider, within the bound.
A program may use at most 64 MiB of HBM per device.

```python
import math
import jax
import jax.numpy as jnp
from jax import lax

C = 768
NB = 8
HID = 768
B = 2
H = 256
W = 512
KH = 128
KW = 128


def place_ends(values, own_key, least, high):
    shape = values.shape
    place = [jax.random.randint(jax.random.fold_in(own_key, axis), (), 0, shape[axis]) for axis in range(len(shape))]
    values = values.at[tuple(place)].set(least)
    longest = shape.index(max(shape))
    place[longest] = (place[longest] + 1) % shape[longest]
    return values.at[tuple(place)].set(high)


def block_levels(rng, shape, shards, smallest, top_value):
    gain = 1.0
    for axis_at, shards_of in shards:
        draws = jax.random.uniform(jax.random.fold_in(jax.random.fold_in(rng, 6), axis_at), (shards_of,), jnp.float32, smallest / len(shards), top_value / len(shards))
        gain = gain * jnp.repeat(jnp.exp(draws), shape[axis_at] // shards_of).reshape((-1,) + (1,) * (len(shape) - 1 - axis_at))
    return gain


def normal_values(key, shape, scale, reach, shards=(), kind=jnp.bfloat16):
    values = scale * jax.random.normal(key, shape, jnp.float32)
    if shards:
        values = values * block_levels(key, shape, shards, -0.22, 0.18)
    return jnp.clip(values, -reach, reach).astype(kind)


def setup_inputs(seed: int = 0) -> dict:
    seeds = jax.random.split(jax.random.key(seed), 8)
    fields = normal_values(seeds[0], (B, H, W, C), 1.0, 6.0, ((1, 32), (2, 8)))
    cotangent = normal_values(seeds[1], (B, H, W, C), 1.0, 6.0, ((1, 32), (2, 8)))
    kept_mask = place_ends((jax.random.randint(seeds[2], (KH, KW, NB), 0, 4) < 3).astype(jnp.int32), jax.random.fold_in(seeds[2], 1), 0, 1)
    w_one = normal_values(seeds[3], (NB, 2, C // NB, HID // NB), (2 * C // NB) ** -0.5, 0.4375, ((0, 8),))
    b_one = normal_values(seeds[4], (NB, 2, HID // NB), 0.5, 3.0, ((0, 8),))
    w_two = normal_values(seeds[5], (NB, 2, HID // NB, C // NB), (2 * HID // NB) ** -0.5, 0.4375, ((0, 8),))
    b_two = normal_values(seeds[6], (NB, 2, C // NB), 0.5, 3.0, ((0, 8),))
    return dict(fields=fields, cotangent=cotangent, kept_mask=kept_mask, w_one=w_one, b_one=b_one, w_two=w_two, b_two=b_two)


def activate(values):
    return values * 0.5 * (1.0 + lax.erf(values * (1.0 / math.sqrt(2.0))))

def activate_slope(values):
    cumulative = 0.5 * (1.0 + lax.erf(values * (1.0 / math.sqrt(2.0))))
    density = jnp.exp(-0.5 * values * values) * (1.0 / math.sqrt(2.0 * math.pi))
    return cumulative + values * density

def wave_tables(lon_cells, kept_w):
    wavenumber = jnp.arange(kept_w, dtype=jnp.int32)
    position = jnp.arange(lon_cells, dtype=jnp.int32)
    angles = (wavenumber[:, None] * position[None, :] % lon_cells).astype(jnp.float32) * (2.0 * math.pi / lon_cells)
    factor = 1.0 / math.sqrt(lon_cells)
    forward = jnp.stack([jnp.cos(angles) * factor, -jnp.sin(angles) * factor], 0)
    weights = jnp.where(wavenumber == 0, 1.0, 2.0).astype(jnp.float32)
    inverse = forward * weights[None, :, None]
    return (forward.astype(jnp.bfloat16), inverse.astype(jnp.bfloat16))

def lat_tables(lat_cells, kept_h):
    wavenumber = jnp.arange(kept_h, dtype=jnp.int32)
    wavenumber = jnp.where(wavenumber < kept_h // 2, wavenumber, wavenumber - kept_h)
    position = jnp.arange(lat_cells, dtype=jnp.int32)
    angles = (wavenumber[:, None] * position[None, :] % lat_cells).astype(jnp.float32) * (2.0 * math.pi / lat_cells)
    factor = 1.0 / math.sqrt(lat_cells)
    cosine = jnp.cos(angles) * factor
    sine = jnp.sin(angles) * factor
    forward = jnp.stack([jnp.stack([cosine, sine], 1), jnp.stack([-sine, cosine], 1)], 0)
    return (forward.astype(jnp.bfloat16), forward.transpose(2, 3, 0, 1).astype(jnp.bfloat16))

def complex_matrix(weights):
    real_part = weights[:, 0]
    imag_part = weights[:, 1]
    upper_rows = jnp.concatenate([real_part, imag_part], 2)
    lower_rows = jnp.concatenate([-imag_part, real_part], 2)
    return jnp.concatenate([upper_rows, lower_rows], 1)

def split_grad(total_grad, first, second):
    real_part = total_grad[:, :first, :second] + total_grad[:, first:, second:]
    imag_part = total_grad[:, :first, second:] - total_grad[:, first:, :second]
    return jnp.stack([real_part, imag_part], 1)

def reference(fields, cotangent, kept_mask, w_one, b_one, w_two, b_two):
    f32 = jnp.float32
    bf16 = jnp.bfloat16
    block_size = C // NB
    block_hidden = HID // NB
    mode_rows = B * KH * KW
    wave_fwd, wave_inv = wave_tables(W, KW)
    lat_fwd, lat_inv = lat_tables(H, KH)

    def to_modes(field_in, matrix):
        spectrum = jnp.einsum('pkw,bhwc->bhpkc', matrix.astype(f32), field_in.astype(f32)).astype(bf16)
        spectrum = spectrum.astype(f32).reshape(B, H, 2, KW, NB, block_size)
        result = jnp.einsum('qmph,bhpknc->nbmkqc', lat_fwd.astype(f32), spectrum)
        return result.reshape(NB, mode_rows, 2 * block_size)

    def to_fields(mode_vals, matrix):
        shaped = mode_vals.astype(f32).reshape(NB, B, KH, KW, 2, block_size)
        spectrum = jnp.einsum('phqm,nbmkqc->bhpknc', lat_inv.astype(f32), shaped).astype(bf16)
        spectrum = spectrum.reshape(B, H, 2, KW, C).astype(f32)
        return jnp.einsum('pkw,bhpkc->bhwc', matrix.astype(f32), spectrum).astype(bf16)
    live_mask = jnp.broadcast_to(kept_mask.astype(f32).transpose(2, 0, 1)[:, None], (NB, B, KH, KW))
    live_mask = live_mask.reshape(NB, mode_rows, 1)
    first = complex_matrix(w_one).astype(f32)
    second = complex_matrix(w_two).astype(f32)
    mode_in = to_modes(fields, wave_fwd).astype(bf16)
    pre_act = jnp.einsum('nrd,nde->nre', mode_in.astype(f32), first) + b_one.astype(f32).reshape(NB, 1, 2 * block_hidden)
    hidden = activate(pre_act).astype(bf16)
    out_modes = live_mask * (jnp.einsum('nre,ned->nrd', hidden.astype(f32), second) + b_two.astype(f32).reshape(NB, 1, 2 * block_size))
    out_modes = out_modes.astype(bf16)
    wave_y = to_fields(out_modes, wave_inv)
    mixed = (fields.astype(f32) + wave_y.astype(f32)).astype(bf16)
    grad_modes = (live_mask * to_modes(cotangent, wave_inv)).astype(bf16)
    grad_hidden = jnp.einsum('nrd,ned->nre', grad_modes.astype(f32), second)
    grad_pre = (grad_hidden * activate_slope(pre_act)).astype(bf16)
    grad_in = jnp.einsum('nre,nde->nrd', grad_pre.astype(f32), first).astype(bf16)
    wave_g = to_fields(grad_in, wave_fwd)
    grad_fields = (cotangent.astype(f32) + wave_g.astype(f32)).astype(bf16)
    factor = 1.0 / math.sqrt(mode_rows)
    total_one = jnp.einsum('nrd,nre->nde', mode_in.astype(f32), grad_pre.astype(f32))
    total_two = jnp.einsum('nre,nrd->ned', hidden.astype(f32), grad_modes.astype(f32))
    grad_w_one = split_grad(total_one, block_size, block_hidden) * factor
    grad_b_one = lax.optimization_barrier(jnp.sum(grad_pre.astype(f32), 1)).reshape(NB, 2, block_hidden) * factor
    grad_w_two = split_grad(total_two, block_hidden, block_size) * factor
    grad_b_two = lax.optimization_barrier(jnp.sum(grad_modes.astype(f32), 1)).reshape(NB, 2, block_size) * factor
    return (mixed, grad_fields, grad_w_one, grad_b_one, grad_w_two, grad_b_two)
```

```python
import functools
import math

import jax
import jax.numpy as jnp
import numpy as np
from jax import lax
from jax.experimental import pallas as pl
from jax.experimental.pallas import tpu as pltpu
from jax.sharding import PartitionSpec as P

MESH = pl.DeviceIdType.MESH
BF16 = jnp.bfloat16
F32 = jnp.float32
CHUNKS = 3
AUX = 16


def wave_tables(lon_cells, kept_w):
    wavenumber = np.arange(kept_w, dtype=np.int32)
    position = np.arange(lon_cells, dtype=np.int32)
    angles = (wavenumber[:, None] * position[None, :] % lon_cells).astype(np.float32) * np.float32(
        2.0 * math.pi / lon_cells
    )
    factor = np.float32(1.0 / math.sqrt(lon_cells))
    forward = np.stack([np.cos(angles) * factor, -np.sin(angles) * factor], 0)
    weights = np.where(wavenumber == 0, 1.0, 2.0).astype(np.float32)
    inverse = forward * weights[None, :, None]
    return (forward.astype(BF16), inverse.astype(BF16))


def lat_tables(lat_cells, kept_h):
    wavenumber = np.arange(kept_h, dtype=np.int32)
    wavenumber = np.where(wavenumber < kept_h // 2, wavenumber, wavenumber - kept_h)
    position = np.arange(lat_cells, dtype=np.int32)
    angles = (wavenumber[:, None] * position[None, :] % lat_cells).astype(np.float32) * np.float32(
        2.0 * math.pi / lat_cells
    )
    factor = np.float32(1.0 / math.sqrt(lat_cells))
    cosine = np.cos(angles) * factor
    sine = np.sin(angles) * factor
    forward = np.stack([np.stack([cosine, sine], 1), np.stack([-sine, cosine], 1)], 0)
    return forward.astype(BF16)


def ordered_tables(lat_count, lon_cells):
    kept_w = 4 * lat_count
    lat_cells = 8 * lat_count
    forward, inverse = wave_tables(lon_cells, kept_w)

    def rows(table):
        shaped = table.reshape(2, lat_count, 2, 2, lon_cells)
        return np.ascontiguousarray(shaped.transpose(2, 3, 1, 0, 4).reshape(8 * lat_count, lon_cells))

    forward, inverse = rows(forward), rows(inverse)
    lat = lat_tables(lat_cells, lat_cells // 2)
    lat = np.ascontiguousarray(lat.transpose(0, 1, 3, 2).reshape(lat_cells, 2 * lat_cells))
    return (
        forward,
        inverse,
        np.ascontiguousarray(forward.T),
        np.ascontiguousarray(inverse.T),
        lat,
        np.ascontiguousarray(lat.T),
    )


def dot(left, right):
    return jnp.dot(left, right, preferred_element_type=F32)


def dot_nt(left, right):
    return lax.dot_general(left, right, (((1,), (1,)), ((), ())), preferred_element_type=F32)


def dot_tn(left, right):
    return lax.dot_general(left, right, (((0,), (0,)), ((), ())), preferred_element_type=F32)


def arrived(ref, sem):
    pltpu.make_async_copy(ref, ref, sem).wait()


def kernel(
    lat_count,
    block,
    scale,
    fields,
    cotangent,
    w_one,
    w_two,
    aux,
    tables_in,
    wave_y,
    wave_g,
    grads,
    tables,
    rows_in,
    own_spec,
    sib_spec,
    lat_out,
    lat_in,
    modes,
    back_modes,
    back_out,
    back_in,
    sib_back,
    wave_spec,
    wave_rows,
    pack,
    packs,
    place,
    perm_out,
    perm_in,
    first,
    second,
    bias,
    mask,
    hidden,
    slope,
    grad_pre,
    grad_send,
    grad_parts,
    grad_sum,
    grad_slots,
    grad_own,
    grad_all,
    table_sem,
    x_send,
    x_recv,
    sib_send,
    sib_recv,
    lat_send,
    lat_recv,
    back_send,
    back_recv,
    sib_back_send,
    sib_back_recv,
    y_send,
    y_recv,
    pack_send,
    pack_recv,
    grad_send_sem,
    grad_recv_sem,
):
    n_lat = lat_count
    lat = lax.axis_index("lat")
    lon = lax.axis_index("lon")
    core = lax.rem(lon, 2)
    sibling = lon + 1 - 2 * core
    chip = lax.div(lon, 2)
    sample = lax.rem(chip, 2)
    half = lax.div(chip, 2)
    spec_rows = 2 * n_lat
    core_rows = 8 * n_lat
    kept = 4 * n_lat
    width = rows_in.shape[-1]
    chunks = rows_in.shape[1]
    span = chunks * width
    local_w = fields.shape[2]
    group = lax.rem(lon, 4)
    group_base = lon - group

    def lon_peer(i):
        return lax.rem(lon + i, 8)

    def lat_peer(i):
        return lax.rem(lat + i, n_lat)

    def remote(src, dst, send_sem, recv_sem, lat_to, lon_to):
        return pltpu.make_async_remote_copy(
            src_ref=src,
            dst_ref=dst,
            send_sem=send_sem,
            recv_sem=recv_sem,
            device_id=(lat_to, lon_to),
            device_id_type=MESH,
        )

    barrier = pltpu.get_barrier_semaphore()

    def greet_lon(i, carry):
        pl.semaphore_signal(barrier, inc=1, device_id=(lat, lon_peer(i)), device_id_type=MESH)
        return carry

    def greet_lat(i, carry):
        pl.semaphore_signal(barrier, inc=1, device_id=(lat_peer(i), lon), device_id_type=MESH)
        return carry

    lax.fori_loop(1, 8, greet_lon, 0)
    lax.fori_loop(1, n_lat, greet_lat, 0)
    for at in range(len(tables)):
        pltpu.make_async_copy(tables_in[at], tables[at], table_sem.at[at]).start()
    pl.semaphore_wait(barrier, 7 + n_lat - 1)

    def x_block(source, owner, chunk):
        owner_core = lax.rem(owner, 2)
        owner_chip = lax.div(owner, 2)
        lanes = pl.multiple_of(lax.div(owner_chip, 2) * span + chunk * width, 128)
        return source.at[
            lax.rem(owner_chip, 2), pl.ds(owner_core * 4, 4), :, pl.ds(lanes, width)
        ]

    def x_slot(which, chunk):
        here = pl.multiple_of(lon * local_w, local_w)
        return rows_in.at[which, chunk, :, pl.ds(here, local_w), :]

    def send_rows(which, chunk):
        source = (fields, cotangent)[which]

        def step(i, carry):
            to = lon_peer(i)
            remote(
                x_block(source, to, chunk),
                x_slot(which, chunk),
                x_send.at[which, chunk],
                x_recv.at[which, chunk],
                lat,
                to,
            ).start()
            return carry

        lax.fori_loop(1, 8, step, 0)
        pltpu.make_async_copy(
            x_block(source, lon, chunk), x_slot(which, chunk), x_recv.at[which, chunk]
        ).start()

    for chunk in range(chunks):
        send_rows(0, chunk)

    pack[...] = jnp.zeros_like(pack)
    for at in range(2):
        pack[at * block : (at + 1) * block, :block] = w_one[at]
        pack[(2 + at) * block : (3 + at) * block, :block] = w_two[at]
    pack[4 * block :, :] = aux[...]

    def send_pack(i, carry):
        to = group_base + lax.rem(group + i, 4)
        remote(pack, packs.at[group], pack_send, pack_recv, lat, to).start()
        return carry

    lax.fori_loop(1, 4, send_pack, 0)
    pltpu.make_async_copy(pack, packs.at[group], pack_recv).start()

    for chunk in range(chunks):
        send_rows(1, chunk)

    total_rows = 16 * n_lat
    out_row = lax.broadcasted_iota(jnp.int32, (total_rows, total_rows), 0)
    in_row = lax.broadcasted_iota(jnp.int32, (total_rows, total_rows), 1)

    def spread(row):
        return ((row >> 1) & 7) * spec_rows + (row >> 4) * 2 + (row & 1)

    perm_out[...] = (spread(out_row) == in_row).astype(F32).astype(BF16)
    perm_in[...] = (spread(in_row) == out_row).astype(F32).astype(BF16)
    lane_in = lax.broadcasted_iota(jnp.int32, (128, span), 0)
    lane_out = lax.broadcasted_iota(jnp.int32, (128, span), 1)
    for n in range(4):
        place[n] = (
            jnp.where(lane_in < block, lane_in + n * block, -1) == lane_out
        ).astype(F32).astype(BF16)

    for at in range(len(tables)):
        arrived(tables[at], table_sem.at[at])
    wave_fwd, wave_inv, wave_fwd_t, wave_inv_t, lat_fwd, lat_inv = tables

    def wave_in(which, chunk):
        matrix = (wave_fwd, wave_inv)[which]
        arrived(rows_in.at[which, chunk], x_recv.at[which, chunk])

        def step(hh, carry):
            block_rows = rows_in[which, chunk, hh]
            own_rows = pl.multiple_of(core * kept, kept)
            sib_rows = pl.multiple_of((1 - core) * kept, kept)
            own = dot(matrix[pl.ds(own_rows, kept), :], block_rows).astype(BF16)
            sib = dot(matrix[pl.ds(sib_rows, kept), :], block_rows).astype(BF16)
            own_at = pl.multiple_of(core * core_rows + hh * spec_rows, spec_rows)
            sib_at = pl.multiple_of(hh * spec_rows, spec_rows)
            for k2 in range(2):
                lanes = slice(k2 * width, (k2 + 1) * width)
                piece = slice(k2 * spec_rows, (k2 + 1) * spec_rows)
                own_spec[which, chunk, pl.ds(own_at, spec_rows), lanes] = own[piece]
                sib_spec[which, chunk, pl.ds(sib_at, spec_rows), lanes] = sib[piece]
            return carry

        lax.fori_loop(0, 4, step, 0)
        there = pl.multiple_of(core * core_rows, core_rows)
        remote(
            sib_spec.at[which, chunk],
            own_spec.at[which, chunk, pl.ds(there, core_rows), :],
            sib_send.at[which, chunk],
            sib_recv.at[which, chunk],
            lat,
            sibling,
        ).start()

    def send_lat(source, target, send_sem, recv_sem, which, chunk):
        def rows_of(ref, at):
            return ref.at[which, chunk, pl.ds(pl.multiple_of(at * 16, 16), 16), :]

        def step(i, carry):
            to = lat_peer(i)
            remote(
                rows_of(source, to),
                rows_of(target, lat),
                send_sem.at[which, chunk],
                recv_sem.at[which, chunk],
                to,
                lon,
            ).start()
            return carry

        lax.fori_loop(1, n_lat, step, 0)
        pltpu.make_async_copy(
            rows_of(source, lat), rows_of(target, lat), recv_sem.at[which, chunk]
        ).start()

    def spectra_out(which, chunk):
        arrived(sib_spec.at[which, chunk], sib_recv.at[which, chunk])
        lat_out[which, chunk] = dot(perm_out[...], own_spec[which, chunk]).astype(BF16)
        send_lat(lat_out, lat_in, lat_send, lat_recv, which, chunk)

    def into_modes(which):
        for chunk in range(chunks):
            arrived(lat_in.at[which, chunk], lat_recv.at[which, chunk])
            result = dot(lat_fwd[...], lat_in[which, chunk]).astype(BF16)
            for q in range(2):
                for k2 in range(2):
                    modes[
                        which,
                        k2 * kept : (k2 + 1) * kept,
                        q * span + chunk * width : q * span + (chunk + 1) * width,
                    ] = result[q * kept : (q + 1) * kept, k2 * width : (k2 + 1) * width]

    def from_modes(which, values):
        back_modes[which] = values
        for chunk in range(chunks):
            rows = []
            for q in range(2):
                lanes = slice(q * span + chunk * width, q * span + (chunk + 1) * width)
                rows.append(
                    jnp.concatenate(
                        [back_modes[which, :kept, lanes], back_modes[which, kept:, lanes]], 1
                    )
                )
            spectrum = jnp.concatenate(rows, 0)
            back_out[which, chunk] = dot(lat_inv[...], spectrum).astype(BF16)
            send_lat(back_out, back_in, back_send, back_recv, which, chunk)

    def back_rows(which, chunk):
        arrived(back_in.at[which, chunk], back_recv.at[which, chunk])
        own_rows = pl.multiple_of(core * core_rows, core_rows)
        sib_rows = pl.multiple_of((1 - core) * core_rows, core_rows)
        received = back_in[which, chunk]
        sib_back[which, chunk] = dot(perm_in[pl.ds(sib_rows, core_rows), :], received).astype(BF16)
        remote(
            sib_back.at[which, chunk],
            wave_spec.at[which, chunk, core],
            sib_back_send.at[which, chunk],
            sib_back_recv.at[which, chunk],
            lat,
            sibling,
        ).start()
        wave_spec[which, chunk, core] = dot(
            perm_in[pl.ds(own_rows, core_rows), :], received
        ).astype(BF16)

    def wave_out(which, chunk):
        matrix = (wave_inv_t, wave_fwd_t)[which]
        target = (wave_y, wave_g)[which]
        arrived(sib_back.at[which, chunk], sib_back_recv.at[which, chunk])

        def step(hh, carry):
            at = pl.ds(pl.multiple_of(hh * spec_rows, spec_rows), spec_rows)
            spectrum = jnp.concatenate(
                [
                    wave_spec[which, chunk, side, at, k2 * width : (k2 + 1) * width]
                    for side in range(2)
                    for k2 in range(2)
                ],
                0,
            )
            wave_rows[which, chunk, hh] = dot(matrix[...], spectrum).astype(BF16)
            return carry

        lax.fori_loop(0, 4, step, 0)
        lanes = pl.multiple_of(half * span + chunk * width, 128)
        slot = target.at[sample, pl.ds(core * 4, 4), :, pl.ds(lanes, width)]

        def columns(to):
            return wave_rows.at[
                which, chunk, :, pl.ds(pl.multiple_of(to * local_w, local_w), local_w), :
            ]

        def send(i, carry):
            to = lon_peer(i)
            remote(columns(to), slot, y_send.at[which], y_recv.at[which], lat, to).start()
            return carry

        lax.fori_loop(1, 8, send, 0)
        pltpu.make_async_copy(columns(lon), slot, y_recv.at[which]).start()

    def build_weights():
        arrived(packs, pack_recv)
        for n in range(4):
            rows = slice(n * block, (n + 1) * block)
            below = slice(span + n * block, span + (n + 1) * block)
            for at, target in ((0, first), (2, second)):
                real = dot(packs[n, at * block : (at + 1) * block, :], place[n])
                imag = dot(packs[n, (at + 1) * block : (at + 2) * block, :], place[n])
                target[rows, :span] = real.astype(BF16)
                target[rows, span:] = imag.astype(BF16)
                target[below, :span] = (-imag).astype(BF16)
                target[below, span:] = real.astype(BF16)
        extra = [packs[n, 4 * block :, :] for n in range(4)]
        spread_bias = sum(dot(extra[n], place[n]) for n in range(4))
        bias[0:1, :span] = spread_bias[0:1]
        bias[0:1, span:] = spread_bias[1:2]
        bias[1:2, :span] = spread_bias[2:3]
        bias[1:2, span:] = spread_bias[3:4]
        stacked = jnp.concatenate(extra, 0)
        row = lax.broadcasted_iota(jnp.int32, (4 * AUX, span), 0)
        lane = lax.broadcasted_iota(jnp.int32, (4 * AUX, span), 1)
        low = (row >> 4) * block
        inside = (lane >= low) & (lane < low + block)
        for k2 in range(2):
            chosen = inside & ((row & (AUX - 1)) == 4 + 2 * core + k2)
            kept_here = dot_tn(stacked, chosen.astype(F32).astype(BF16))[:kept]
            mask[k2 * kept : (k2 + 1) * kept, :span] = kept_here
            mask[k2 * kept : (k2 + 1) * kept, span:] = kept_here

    def mlp_forward():
        pre = dot(modes[0], first[...]) + bias[0:1, :]
        cumulative = 0.5 * (1.0 + lax.erf(pre * (1.0 / math.sqrt(2.0))))
        density = jnp.exp(-0.5 * pre * pre) * (1.0 / math.sqrt(2.0 * math.pi))
        hidden[...] = (pre * cumulative).astype(BF16)
        slope[...] = cumulative + pre * density
        output = dot(hidden[...], second[...]) + bias[1:2, :]
        return (mask[...] * output).astype(BF16)

    def mlp_backward():
        modes[1] = (mask[...] * modes[1].astype(F32)).astype(BF16)
        grad_hidden = dot_nt(modes[1], second[...])
        grad_pre[...] = (grad_hidden * slope[...]).astype(BF16)
        return dot_nt(grad_pre[...], first[...]).astype(BF16)

    def grad_partials():
        sums = []
        for at, (left, right) in enumerate(((modes.at[0], grad_pre), (hidden, modes.at[1]))):
            total = dot_tn(left[...], right[...])
            parts = (
                total[:span, :span] + total[span:, span:],
                total[:span, span:] - total[span:, :span],
            )
            for which, part in enumerate(parts):
                part = part.astype(BF16)
                for n in range(4):
                    grad_send[
                        n, (2 * at + which) * block : (2 * at + which + 1) * block, :
                    ] = dot_nt(part[n * block : (n + 1) * block, :], place[n]).astype(BF16)
            summed = jnp.sum(right[...].astype(F32), 0, keepdims=True)
            sums += [summed[:, :span], summed[:, span:]]
        row = lax.broadcasted_iota(jnp.int32, (AUX, span), 0)
        stacked = jnp.zeros((AUX, span), F32)
        for at, value in enumerate(sums):
            stacked = jnp.where(row == at, value, stacked)
        stacked = stacked.astype(BF16)
        tail = grad_send.shape[1] - 4 * block - AUX
        for n in range(4):
            grad_send[n, 4 * block : 4 * block + AUX, :] = dot_nt(stacked, place[n]).astype(BF16)
            if tail:
                grad_send[n, 4 * block + AUX :, :] = jnp.zeros((tail, 128), BF16)

        def step(i, carry):
            to = lax.rem(group + i, 4)
            remote(
                grad_send.at[to],
                grad_parts.at[group],
                grad_send_sem.at[0],
                grad_recv_sem.at[0],
                lat,
                group_base + to,
            ).start()
            return carry

        lax.fori_loop(1, 4, step, 0)
        pltpu.make_async_copy(
            grad_send.at[group], grad_parts.at[group], grad_recv_sem.at[0]
        ).start()

    share = grad_slots.shape[1]

    def share_of(ref, at):
        return ref.at[pl.ds(pl.multiple_of(at * share, 16), share), :]

    def grad_scatter():
        arrived(grad_parts, grad_recv_sem.at[0])
        grad_sum[...] = sum(grad_parts[n].astype(F32) for n in range(4)).astype(BF16)

        def step(i, carry):
            to = lat_peer(i)
            remote(
                share_of(grad_sum, to),
                grad_slots.at[lat],
                grad_send_sem.at[1],
                grad_recv_sem.at[1],
                to,
                lon,
            ).start()
            return carry

        lax.fori_loop(1, n_lat, step, 0)
        pltpu.make_async_copy(
            share_of(grad_sum, lat), grad_slots.at[lat], grad_recv_sem.at[1]
        ).start()

    def grad_gather():
        arrived(grad_slots, grad_recv_sem.at[1])
        grad_own[...] = jnp.sum(grad_slots[...].astype(F32), 0).astype(BF16)

        def step(i, carry):
            remote(
                grad_own,
                share_of(grad_all, lat),
                grad_send_sem.at[2],
                grad_recv_sem.at[2],
                lat_peer(i),
                lon,
            ).start()
            return carry

        lax.fori_loop(1, n_lat, step, 0)
        pltpu.make_async_copy(grad_own, share_of(grad_all, lat), grad_recv_sem.at[2]).start()

    def grad_finish():
        arrived(grad_all, grad_recv_sem.at[2])
        grads[...] = grad_all[...].astype(F32) * scale

    for chunk in range(chunks):
        wave_in(0, chunk)
        spectra_out(0, chunk)
    build_weights()
    wave_in(1, 0)
    spectra_out(1, 0)
    into_modes(0)
    from_modes(0, mlp_forward())
    for chunk in range(1, chunks):
        wave_in(1, chunk)
        spectra_out(1, chunk)
    for chunk in range(chunks):
        back_rows(0, chunk)
        wave_out(0, chunk)
    into_modes(1)
    from_modes(1, mlp_backward())
    grad_partials()
    grad_scatter()
    grad_gather()
    for chunk in range(chunks):
        back_rows(1, chunk)
        wave_out(1, chunk)
    grad_finish()

    arrived(wave_y, y_recv.at[0])
    arrived(wave_g, y_recv.at[1])
    for which in range(2):
        for chunk in range(chunks):
            arrived(rows_in.at[which, chunk, :, : 7 * local_w, :], x_send.at[which, chunk])
            arrived(sib_spec.at[which, chunk], sib_send.at[which, chunk])
            arrived(lat_out.at[which, chunk, : 16 * (n_lat - 1), :], lat_send.at[which, chunk])
            arrived(back_out.at[which, chunk, : 16 * (n_lat - 1), :], back_send.at[which, chunk])
            arrived(sib_back.at[which, chunk], sib_back_send.at[which, chunk])
        arrived(wave_rows.at[which, :, :, : 7 * local_w, :], y_send.at[which])
    arrived(packs.at[:3], pack_send)
    arrived(grad_send.at[:3], grad_send_sem.at[0])
    arrived(grad_slots.at[: n_lat - 1], grad_send_sem.at[1])
    arrived(grad_slots.at[: n_lat - 1], grad_send_sem.at[2])


def per_device(fields, cotangent, kept_mask, w_one, b_one, w_two, b_two):
    lat_count = lax.axis_size("lat")
    lon_count = lax.axis_size("lon")
    samples, _, local_w, channels = fields.shape
    lon_cells = local_w * lon_count
    block = w_one.shape[2]
    span = channels // 2
    width = span // CHUNKS
    kept = 4 * lat_count
    rows = 16 * lat_count
    tables = ordered_tables(lat_count, lon_cells)
    share = -(-(4 * block + AUX) // (16 * lat_count)) * 16
    grad_rows = share * lat_count

    aux = jnp.concatenate(
        [
            jnp.pad(b_one[0].astype(BF16), ((0, 0), (0, 128 - block))),
            jnp.pad(b_two[0].astype(BF16), ((0, 0), (0, 128 - block))),
            jnp.pad(kept_mask[:, :, 0].T.astype(BF16), ((0, 0), (0, 128 - kept))),
            jnp.zeros((AUX - 8, 128), BF16),
        ],
        0,
    )

    vmem = pl.BlockSpec(memory_space=pltpu.VMEM)
    anywhere = pl.BlockSpec(memory_space=pl.ANY)
    dma = pltpu.SemaphoreType.DMA
    scratch = [
        [pltpu.VMEM(table.shape, BF16) for table in tables],
        pltpu.VMEM((2, CHUNKS, 4, lon_cells, width), BF16),
        pltpu.VMEM((2, CHUNKS, rows, 2 * width), BF16),
        pltpu.VMEM((2, CHUNKS, rows // 2, 2 * width), BF16),
        pltpu.VMEM((2, CHUNKS, rows, 2 * width), BF16),
        pltpu.VMEM((2, CHUNKS, rows, 2 * width), BF16),
        pltpu.VMEM((2, 2 * kept, 2 * span), BF16),
        pltpu.VMEM((2, 2 * kept, 2 * span), BF16),
        pltpu.VMEM((2, CHUNKS, rows, 2 * width), BF16),
        pltpu.VMEM((2, CHUNKS, rows, 2 * width), BF16),
        pltpu.VMEM((2, CHUNKS, rows // 2, 2 * width), BF16),
        pltpu.VMEM((2, CHUNKS, 2, rows // 2, 2 * width), BF16),
        pltpu.VMEM((2, CHUNKS, 4, lon_cells, width), BF16),
        pltpu.VMEM((4 * block + AUX, 128), BF16),
        pltpu.VMEM((4, 4 * block + AUX, 128), BF16),
        pltpu.VMEM((4, 128, span), BF16),
        pltpu.VMEM((rows, rows), BF16),
        pltpu.VMEM((rows, rows), BF16),
        pltpu.VMEM((2 * span, 2 * span), BF16),
        pltpu.VMEM((2 * span, 2 * span), BF16),
        pltpu.VMEM((8, 2 * span), F32),
        pltpu.VMEM((2 * kept, 2 * span), F32),
        pltpu.VMEM((2 * kept, 2 * span), BF16),
        pltpu.VMEM((2 * kept, 2 * span), F32),
        pltpu.VMEM((2 * kept, 2 * span), BF16),
        pltpu.VMEM((4, grad_rows, 128), BF16),
        pltpu.VMEM((4, grad_rows, 128), BF16),
        pltpu.VMEM((grad_rows, 128), BF16),
        pltpu.VMEM((lat_count, share, 128), BF16),
        pltpu.VMEM((share, 128), BF16),
        pltpu.VMEM((grad_rows, 128), BF16),
        dma((len(tables),)),
        dma((2, CHUNKS)),
        dma((2, CHUNKS)),
        dma((2, CHUNKS)),
        dma((2, CHUNKS)),
        dma((2, CHUNKS)),
        dma((2, CHUNKS)),
        dma((2, CHUNKS)),
        dma((2, CHUNKS)),
        dma((2, CHUNKS)),
        dma((2, CHUNKS)),
        dma((2,)),
        dma((2,)),
        dma,
        dma,
        dma((3,)),
        dma((3,)),
    ]
    scale = 1.0 / math.sqrt(samples * kept * kept)
    moved = 4 * samples * fields.shape[1] * local_w * channels * 2
    wave_y, wave_g, grads = pl.pallas_call(
        functools.partial(kernel, lat_count, block, scale),
        out_shape=(
            jax.ShapeDtypeStruct(fields.shape, BF16),
            jax.ShapeDtypeStruct(fields.shape, BF16),
            jax.ShapeDtypeStruct((grad_rows, 128), F32),
        ),
        in_specs=[anywhere, anywhere, vmem, vmem, vmem, [anywhere] * len(tables)],
        out_specs=(anywhere, anywhere, vmem),
        scratch_shapes=scratch,
        compiler_params=pltpu.CompilerParams(
            collective_id=0, has_side_effects=True, vmem_limit_bytes=48 * 1024 * 1024
        ),
        cost_estimate=pl.CostEstimate(
            flops=6 * 10**9, bytes_accessed=moved, transcendentals=4 * kept * span
        ),
    )(
        fields,
        cotangent,
        w_one[0],
        w_two[0],
        aux,
        [jnp.asarray(table) for table in tables],
    )
    mixed = (fields.astype(F32) + wave_y.astype(F32)).astype(BF16)
    grad_fields = (cotangent.astype(F32) + wave_g.astype(F32)).astype(BF16)
    tail = grads[4 * block : 4 * block + 4, :block]
    return (
        mixed,
        grad_fields,
        grads[: 2 * block, :block].reshape(1, 2, block, block),
        tail[:2].reshape(1, 2, block),
        grads[2 * block : 4 * block, :block].reshape(1, 2, block, block),
        tail[2:].reshape(1, 2, block),
    )


def solution(mesh):
    placed = (
        P(None, "lat", "lon", None),
        P(None, "lat", "lon", None),
        P(None, "lat", "lon"),
        P("lon", None, None, None),
        P("lon", None, None),
        P("lon", None, None, None),
        P("lon", None, None),
    )
    return jax.shard_map(
        per_device,
        mesh=mesh,
        in_specs=placed,
        out_specs=(
            P(None, "lat", "lon", None),
            P(None, "lat", "lon", None),
            P("lon", None, None, None),
            P("lon", None, None),
            P("lon", None, None, None),
            P("lon", None, None),
        ),
        check_vma=False,
    )
```

```python
import functools
import math

import jax
import jax.numpy as jnp
import numpy as np
from jax import lax
from jax.experimental import pallas as pl
from jax.experimental.pallas import tpu as pltpu
from jax.sharding import PartitionSpec as P

MESH = pl.DeviceIdType.MESH
BF16 = jnp.bfloat16
F32 = jnp.float32
CHUNKS = 3
AUX = 16


def wave_tables(lon_cells, kept_w):
    wavenumber = np.arange(kept_w, dtype=np.int32)
    position = np.arange(lon_cells, dtype=np.int32)
    angles = (wavenumber[:, None] * position[None, :] % lon_cells).astype(np.float32) * np.float32(
        2.0 * math.pi / lon_cells
    )
    factor = np.float32(1.0 / math.sqrt(lon_cells))
    forward = np.stack([np.cos(angles) * factor, -np.sin(angles) * factor], 0)
    weights = np.where(wavenumber == 0, 1.0, 2.0).astype(np.float32)
    inverse = forward * weights[None, :, None]
    return (forward.astype(BF16), inverse.astype(BF16))


def lat_tables(lat_cells, kept_h):
    wavenumber = np.arange(kept_h, dtype=np.int32)
    wavenumber = np.where(wavenumber < kept_h // 2, wavenumber, wavenumber - kept_h)
    position = np.arange(lat_cells, dtype=np.int32)
    angles = (wavenumber[:, None] * position[None, :] % lat_cells).astype(np.float32) * np.float32(
        2.0 * math.pi / lat_cells
    )
    factor = np.float32(1.0 / math.sqrt(lat_cells))
    cosine = np.cos(angles) * factor
    sine = np.sin(angles) * factor
    forward = np.stack([np.stack([cosine, sine], 1), np.stack([-sine, cosine], 1)], 0)
    return forward.astype(BF16)


def ordered_tables(lat_count, lon_cells):
    kept_w = 4 * lat_count
    lat_cells = 8 * lat_count
    forward, inverse = wave_tables(lon_cells, kept_w)

    def rows(table):
        shaped = table.reshape(2, lat_count, 2, 2, lon_cells)
        return np.ascontiguousarray(shaped.transpose(2, 3, 1, 0, 4).reshape(8 * lat_count, lon_cells))

    forward, inverse = rows(forward), rows(inverse)
    lat = lat_tables(lat_cells, lat_cells // 2)
    lat = np.ascontiguousarray(lat.transpose(0, 1, 3, 2).reshape(lat_cells, 2 * lat_cells))
    return (
        forward,
        inverse,
        np.ascontiguousarray(forward.T),
        np.ascontiguousarray(inverse.T),
        lat,
        np.ascontiguousarray(lat.T),
    )


def dot(left, right):
    return jnp.dot(left, right, preferred_element_type=F32)


def dot_nt(left, right):
    return lax.dot_general(left, right, (((1,), (1,)), ((), ())), preferred_element_type=F32)


def dot_tn(left, right):
    return lax.dot_general(left, right, (((0,), (0,)), ((), ())), preferred_element_type=F32)


def arrived(ref, sem):
    pltpu.make_async_copy(ref, ref, sem).wait()


def kernel(
    lat_count,
    block,
    scale,
    fields,
    cotangent,
    w_one,
    w_two,
    b_one,
    b_two,
    kept_in,
    tables_in,
    wave_y,
    wave_g,
    grads,
    tables,
    weights,
    biases,
    kept_blocks,
    extra_rows,
    rows_in,
    own_spec,
    sib_spec,
    lat_out,
    lat_in,
    modes,
    back_modes,
    back_out,
    back_in,
    sib_back,
    wave_spec,
    wave_rows,
    pack,
    packs,
    place,
    perm_out,
    perm_in,
    first,
    second,
    bias,
    mask,
    hidden,
    slope,
    grad_pre,
    grad_send,
    grad_core,
    grad_pair,
    grad_chip_in,
    grad_sum,
    grad_y,
    grad_y_sum,
    grad_z,
    grad_own,
    grad_z_all,
    grad_all,
    table_sem,
    x_send,
    x_recv,
    sib_send,
    sib_recv,
    lat_send,
    lat_recv,
    back_send,
    back_recv,
    sib_back_send,
    sib_back_recv,
    y_send,
    y_recv,
    pack_send,
    pack_recv,
    grad_send_sem,
    grad_recv_sem,
):
    n_lat = lat_count
    lat = lax.axis_index("lat")
    lon = lax.axis_index("lon")
    core = lax.rem(lon, 2)
    sibling = lon + 1 - 2 * core
    chip = lax.div(lon, 2)
    sample = lax.rem(chip, 2)
    half = lax.div(chip, 2)
    spec_rows = 2 * n_lat
    core_rows = 8 * n_lat
    kept = 4 * n_lat
    width = rows_in.shape[-1]
    chunks = rows_in.shape[1]
    span = chunks * width
    local_w = fields.shape[2]
    group = lax.rem(lon, 4)
    group_base = lon - group

    def lon_peer(i):
        return lax.rem(lon + i, 8)

    def lat_peer(i):
        return lax.rem(lat + i, n_lat)

    def remote(src, dst, send_sem, recv_sem, lat_to, lon_to):
        return pltpu.make_async_remote_copy(
            src_ref=src,
            dst_ref=dst,
            send_sem=send_sem,
            recv_sem=recv_sem,
            device_id=(lat_to, lon_to),
            device_id_type=MESH,
        )

    barrier = pltpu.get_barrier_semaphore()

    def greet_lon(i, carry):
        pl.semaphore_signal(barrier, inc=1, device_id=(lat, lon_peer(i)), device_id_type=MESH)
        return carry

    def greet_lat(i, carry):
        pl.semaphore_signal(barrier, inc=1, device_id=(lat_peer(i), lon), device_id_type=MESH)
        return carry

    lax.fori_loop(1, 8, greet_lon, 0)
    lax.fori_loop(1, n_lat, greet_lat, 0)
    small = (
        (w_one, weights.at[0]),
        (w_two, weights.at[1]),
        (b_one, biases.at[0]),
        (b_two, biases.at[1]),
        (kept_in, kept_blocks),
    )
    loads = [
        pltpu.make_async_copy(source, target, table_sem.at[at])
        for at, (source, target) in enumerate(small + tuple(zip(tables_in, tables)))
    ]
    for load in loads:
        load.start()
    total_rows = 16 * n_lat
    out_row = lax.broadcasted_iota(jnp.int32, (total_rows, total_rows), 0)
    in_row = lax.broadcasted_iota(jnp.int32, (total_rows, total_rows), 1)

    def spread(row):
        return ((row >> 1) & 7) * spec_rows + (row >> 4) * 2 + (row & 1)

    perm_out[...] = (spread(out_row) == in_row).astype(F32).astype(BF16)
    perm_in[...] = (spread(in_row) == out_row).astype(F32).astype(BF16)
    lane_in = lax.broadcasted_iota(jnp.int32, (128, span), 0)
    lane_out = lax.broadcasted_iota(jnp.int32, (128, span), 1)
    for n in range(4):
        place[n] = (
            jnp.where(lane_in < block, lane_in + n * block, -1) == lane_out
        ).astype(F32).astype(BF16)

    for load in loads[: len(small)]:
        load.wait()
    pack[...] = jnp.zeros_like(pack)
    for at in range(2):
        pack[at * block : (at + 1) * block, :block] = weights[0, at]
        pack[(2 + at) * block : (3 + at) * block, :block] = weights[1, at]
    extra_rows[...] = jnp.zeros_like(extra_rows)
    extra_rows[0:2, :block] = biases[0].astype(F32)
    extra_rows[2:4, :block] = biases[1].astype(F32)
    extra_rows[4:8, :kept] = kept_blocks[...].astype(F32)
    pack[4 * block :, :] = extra_rows[...].astype(BF16)

    pl.semaphore_wait(barrier, 7 + n_lat - 1)

    leaving = {}
    coming = {}

    def drained(*key):
        if key in leaving:
            arrived(*leaving.pop(key))

    def received(*key):
        if key in coming:
            arrived(*coming.pop(key))

    def x_block(source, owner, chunk):
        owner_core = lax.rem(owner, 2)
        owner_chip = lax.div(owner, 2)
        lanes = pl.multiple_of(lax.div(owner_chip, 2) * span + chunk * width, 128)
        return source.at[
            lax.rem(owner_chip, 2), pl.ds(owner_core * 4, 4), :, pl.ds(lanes, width)
        ]

    def x_slot(which, chunk):
        here = pl.multiple_of(lon * local_w, local_w)
        return rows_in.at[which, chunk, :, pl.ds(here, local_w), :]

    def send_rows(which, chunk):
        source = (fields, cotangent)[which]

        def step(i, carry):
            to = lon_peer(i)
            remote(
                x_block(source, to, chunk),
                x_slot(which, chunk),
                x_send.at[which, chunk],
                x_recv.at[which, chunk],
                lat,
                to,
            ).start()
            return carry

        lax.fori_loop(1, 8, step, 0)
        pltpu.make_async_copy(
            x_block(source, lon, chunk), x_slot(which, chunk), x_recv.at[which, chunk]
        ).start()
        leaving["x", which, chunk] = (
            rows_in.at[which, chunk, :, : 7 * local_w, :],
            x_send.at[which, chunk],
        )
        coming["x", which, chunk] = (rows_in.at[which, chunk], x_recv.at[which, chunk])

    send_rows(0, 0)

    partner = lon + 2 - 4 * sample
    partner_slot = group + 2 - 4 * sample

    def send_pack():
        for at, to in enumerate((partner, sibling)):
            remote(pack, packs.at[group], pack_send.at[at], pack_recv.at[at], lat, to).start()
            leaving["pack", at] = (pack, pack_send.at[at])
            coming["pack", at] = (pack, pack_recv.at[at])
        pltpu.make_async_copy(pack, packs.at[group], pack_recv.at[3]).start()
        coming["pack", 3] = (pack, pack_recv.at[3])

    def forward_pack():
        received("pack", 0)
        theirs = packs.at[partner_slot]
        remote(theirs, theirs, pack_send.at[2], pack_recv.at[2], lat, sibling).start()
        leaving["pack", 2] = (pack, pack_send.at[2])
        coming["pack", 2] = (pack, pack_recv.at[2])

    for load in loads[len(small) :]:
        load.wait()
    wave_fwd, wave_inv, wave_fwd_t, wave_inv_t, lat_fwd, lat_inv = tables

    def wave_in(which, chunk):
        matrix = (wave_fwd, wave_inv)[which]
        received("x", which, chunk)

        def step(hh, carry):
            block_rows = rows_in[which, chunk, hh]
            own_rows = pl.multiple_of(core * kept, kept)
            sib_rows = pl.multiple_of((1 - core) * kept, kept)
            own = dot(matrix[pl.ds(own_rows, kept), :], block_rows).astype(BF16)
            sib = dot(matrix[pl.ds(sib_rows, kept), :], block_rows).astype(BF16)
            own_at = pl.multiple_of(core * core_rows + hh * spec_rows, spec_rows)
            sib_at = pl.multiple_of(hh * spec_rows, spec_rows)
            for k2 in range(2):
                lanes = slice(k2 * width, (k2 + 1) * width)
                piece = slice(k2 * spec_rows, (k2 + 1) * spec_rows)
                own_spec[which, chunk, pl.ds(own_at, spec_rows), lanes] = own[piece]
                sib_spec[which, chunk, pl.ds(sib_at, spec_rows), lanes] = sib[piece]
            return carry

        lax.fori_loop(0, 4, step, 0)
        there = pl.multiple_of(core * core_rows, core_rows)
        remote(
            sib_spec.at[which, chunk],
            own_spec.at[which, chunk, pl.ds(there, core_rows), :],
            sib_send.at[which, chunk],
            sib_recv.at[which, chunk],
            lat,
            sibling,
        ).start()
        leaving["sib", which, chunk] = (sib_spec.at[which, chunk], sib_send.at[which, chunk])
        coming["sib", which, chunk] = (sib_spec.at[which, chunk], sib_recv.at[which, chunk])

    def send_lat(name, source, target, send_sem, recv_sem, which, chunk):
        def rows_of(ref, at):
            return ref.at[which, chunk, pl.ds(pl.multiple_of(at * 16, 16), 16), :]

        def step(i, carry):
            to = lat_peer(i)
            remote(
                rows_of(source, to),
                rows_of(target, lat),
                send_sem.at[which, chunk],
                recv_sem.at[which, chunk],
                to,
                lon,
            ).start()
            return carry

        lax.fori_loop(1, n_lat, step, 0)
        pltpu.make_async_copy(
            rows_of(source, lat), rows_of(target, lat), recv_sem.at[which, chunk]
        ).start()
        leaving[name, which, chunk] = (
            source.at[which, chunk, : 16 * (n_lat - 1), :],
            send_sem.at[which, chunk],
        )
        coming[name, which, chunk] = (target.at[which, chunk], recv_sem.at[which, chunk])

    def spectra_out(which, chunk):
        received("sib", which, chunk)
        lat_out[which, chunk] = dot(perm_out[...], own_spec[which, chunk]).astype(BF16)
        send_lat("lat", lat_out, lat_in, lat_send, lat_recv, which, chunk)

    def into_modes(which):
        for chunk in range(chunks):
            received("lat", which, chunk)
            result = dot(lat_fwd[...], lat_in[which, chunk]).astype(BF16)
            for q in range(2):
                for k2 in range(2):
                    modes[
                        which,
                        k2 * kept : (k2 + 1) * kept,
                        q * span + chunk * width : q * span + (chunk + 1) * width,
                    ] = result[q * kept : (q + 1) * kept, k2 * width : (k2 + 1) * width]

    def from_modes(which, values):
        back_modes[which] = values
        for chunk in range(chunks):
            rows = []
            for q in range(2):
                lanes = slice(q * span + chunk * width, q * span + (chunk + 1) * width)
                rows.append(
                    jnp.concatenate(
                        [back_modes[which, :kept, lanes], back_modes[which, kept:, lanes]], 1
                    )
                )
            spectrum = jnp.concatenate(rows, 0)
            back_out[which, chunk] = dot(lat_inv[...], spectrum).astype(BF16)

    def send_back(which, chunk):
        send_lat("back", back_out, back_in, back_send, back_recv, which, chunk)

    def back_rows(which, chunk):
        received("back", which, chunk)
        own_rows = pl.multiple_of(core * core_rows, core_rows)
        sib_rows = pl.multiple_of((1 - core) * core_rows, core_rows)
        landed = back_in[which, chunk]
        sib_back[which, chunk] = dot(perm_in[pl.ds(sib_rows, core_rows), :], landed).astype(BF16)
        remote(
            sib_back.at[which, chunk],
            wave_spec.at[which, chunk, core],
            sib_back_send.at[which, chunk],
            sib_back_recv.at[which, chunk],
            lat,
            sibling,
        ).start()
        block_of = sib_back.at[which, chunk]
        leaving["sib_back", which, chunk] = (block_of, sib_back_send.at[which, chunk])
        coming["sib_back", which, chunk] = (block_of, sib_back_recv.at[which, chunk])
        wave_spec[which, chunk, core] = dot(
            perm_in[pl.ds(own_rows, core_rows), :], landed
        ).astype(BF16)

    def wave_out(which, chunk):
        matrix = (wave_inv_t, wave_fwd_t)[which]
        target = (wave_y, wave_g)[which]
        received("sib_back", which, chunk)

        def step(hh, carry):
            at = pl.ds(pl.multiple_of(hh * spec_rows, spec_rows), spec_rows)
            spectrum = jnp.concatenate(
                [
                    wave_spec[which, chunk, side, at, k2 * width : (k2 + 1) * width]
                    for side in range(2)
                    for k2 in range(2)
                ],
                0,
            )
            wave_rows[which, chunk, hh] = dot(matrix[...], spectrum).astype(BF16)
            return carry

        lax.fori_loop(0, 4, step, 0)
        lanes = pl.multiple_of(half * span + chunk * width, 128)
        slot = target.at[sample, pl.ds(core * 4, 4), :, pl.ds(lanes, width)]

        def columns(to):
            return wave_rows.at[
                which, chunk, :, pl.ds(pl.multiple_of(to * local_w, local_w), local_w), :
            ]

        def send(i, carry):
            to = lon_peer(i)
            remote(
                columns(to), slot, y_send.at[which, chunk], y_recv.at[which, chunk], lat, to
            ).start()
            return carry

        lax.fori_loop(1, 8, send, 0)
        pltpu.make_async_copy(columns(lon), slot, y_recv.at[which, chunk]).start()
        leaving["y", which, chunk] = (
            wave_rows.at[which, chunk, :, : 7 * local_w, :],
            y_send.at[which, chunk],
        )
        coming["y", which, chunk] = (
            target.at[:, :, :, : 2 * width],
            y_recv.at[which, chunk],
        )

    def build_weights():
        for at in range(1, 4):
            received("pack", at)
        for n in range(4):
            rows = slice(n * block, (n + 1) * block)
            below = slice(span + n * block, span + (n + 1) * block)
            for at, target in ((0, first), (2, second)):
                real = dot(packs[n, at * block : (at + 1) * block, :], place[n])
                imag = dot(packs[n, (at + 1) * block : (at + 2) * block, :], place[n])
                target[rows, :span] = real.astype(BF16)
                target[rows, span:] = imag.astype(BF16)
                target[below, :span] = (-imag).astype(BF16)
                target[below, span:] = real.astype(BF16)
        extra = [packs[n, 4 * block :, :] for n in range(4)]
        spread_bias = sum(dot(extra[n], place[n]) for n in range(4))
        bias[0:1, :span] = spread_bias[0:1]
        bias[0:1, span:] = spread_bias[1:2]
        bias[1:2, :span] = spread_bias[2:3]
        bias[1:2, span:] = spread_bias[3:4]
        stacked = jnp.concatenate(extra, 0)
        row = lax.broadcasted_iota(jnp.int32, (4 * AUX, span), 0)
        lane = lax.broadcasted_iota(jnp.int32, (4 * AUX, span), 1)
        low = (row >> 4) * block
        inside = (lane >= low) & (lane < low + block)
        for k2 in range(2):
            chosen = inside & ((row & (AUX - 1)) == 4 + 2 * core + k2)
            kept_here = dot_tn(stacked, chosen.astype(F32).astype(BF16))[:kept]
            mask[k2 * kept : (k2 + 1) * kept, :span] = kept_here
            mask[k2 * kept : (k2 + 1) * kept, span:] = kept_here

    def mlp_forward():
        pre = dot(modes[0], first[...]) + bias[0:1, :]
        cumulative = 0.5 * (1.0 + lax.erf(pre * (1.0 / math.sqrt(2.0))))
        density = jnp.exp(-0.5 * pre * pre) * (1.0 / math.sqrt(2.0 * math.pi))
        hidden[...] = (pre * cumulative).astype(BF16)
        slope[...] = cumulative + pre * density
        output = dot(hidden[...], second[...]) + bias[1:2, :]
        return (mask[...] * output).astype(BF16)

    def mlp_backward():
        modes[1] = (mask[...] * modes[1].astype(F32)).astype(BF16)
        grad_hidden = dot_nt(modes[1], second[...])
        grad_pre[...] = (grad_hidden * slope[...]).astype(BF16)
        return dot_nt(grad_pre[...], first[...]).astype(BF16)

    def grad_partials():
        sums = []
        for at, (left, right) in enumerate(((modes.at[0], grad_pre), (hidden, modes.at[1]))):
            total = dot_tn(left[...], right[...])
            parts = (
                total[:span, :span] + total[span:, span:],
                total[:span, span:] - total[span:, :span],
            )
            for which, part in enumerate(parts):
                part = part.astype(BF16)
                for n in range(4):
                    grad_send[
                        n % 2, n // 2, (2 * at + which) * block : (2 * at + which + 1) * block, :
                    ] = dot_nt(part[n * block : (n + 1) * block, :], place[n]).astype(BF16)
            summed = jnp.sum(right[...].astype(F32), 0, keepdims=True)
            sums += [summed[:, :span], summed[:, span:]]
        row = lax.broadcasted_iota(jnp.int32, (AUX, span), 0)
        stacked = jnp.zeros((AUX, span), F32)
        for at, value in enumerate(sums):
            stacked = jnp.where(row == at, value, stacked)
        stacked = stacked.astype(BF16)
        tail = grad_send.shape[2] - 4 * block - AUX
        for n in range(4):
            grad_send[n % 2, n // 2, 4 * block : 4 * block + AUX, :] = dot_nt(
                stacked, place[n]
            ).astype(BF16)
            if tail:
                grad_send[n % 2, n // 2, 4 * block + AUX :, :] = jnp.zeros((tail, 128), BF16)

        grad_copy("core", grad_send.at[1 - core], grad_core, 0, lat, sibling)

    def grad_copy(key, source, target, at, lat_to, lon_to):
        remote(source, target, grad_send_sem.at[at], grad_recv_sem.at[at], lat_to, lon_to).start()
        leaving[key,] = (source, grad_send_sem.at[at])
        coming[key,] = (target, grad_recv_sem.at[at])

    def grad_exchange(key, source_of, target, slot, count, at, to_lat):
        def step(i, carry):
            to = lax.rem(slot + i, count)
            remote(
                source_of(to),
                target.at[slot],
                grad_send_sem.at[at],
                grad_recv_sem.at[at],
                to_lat(to),
                lon,
            ).start()
            return carry

        lax.fori_loop(1, count, step, 0)
        pltpu.make_async_copy(source_of(slot), target.at[slot], grad_recv_sem.at[at]).start()
        leaving[key,] = (target.at[: count - 1], grad_send_sem.at[at])
        coming[key,] = (target, grad_recv_sem.at[at])

    n_z, n_y = grad_z.shape[0], grad_y.shape[0]
    z, y = lax.div(lat, n_y), lax.rem(lat, n_y)
    z_share, y_share = grad_z.shape[1], grad_y.shape[1]

    def along_z(to):
        return to * n_y + y

    def along_y(to):
        return z * n_y + to

    def grad_chip():
        received("core")
        grad_pair[...] = (grad_send[core].astype(F32) + grad_core[...].astype(F32)).astype(BF16)
        grad_copy("chip", grad_pair.at[1 - sample], grad_chip_in, 1, lat, partner)

    def grad_over_y():
        received("chip")
        grad_sum[...] = (grad_pair[sample].astype(F32) + grad_chip_in[...].astype(F32)).astype(BF16)

        def part(to):
            return grad_sum.at[pl.ds(pl.multiple_of(to * y_share, 16), y_share), :]

        grad_exchange("y_sum", part, grad_y, y, n_y, 2, along_y)

    def grad_over_z():
        received("y_sum")
        grad_y_sum[...] = jnp.sum(grad_y[...].astype(F32), 0).astype(BF16)

        def part(to):
            return grad_y_sum.at[pl.ds(pl.multiple_of(to * z_share, 16), z_share), :]

        grad_exchange("z_sum", part, grad_z, z, n_z, 3, along_z)

    def grad_back_z():
        received("z_sum")
        grad_own[...] = jnp.sum(grad_z[...].astype(F32), 0).astype(BF16)
        grad_exchange("z_all", lambda to: grad_own, grad_z_all, z, n_z, 4, along_z)

    def grad_back_y():
        received("z_all")
        grad_exchange("y_all", lambda to: grad_z_all, grad_all, y, n_y, 5, along_y)

    def grad_finish():
        received("y_all")
        for part in range(n_y):
            for piece in range(n_z):
                low = part * y_share + piece * z_share
                grads[low : low + z_share, :] = grad_all[part, piece].astype(F32) * scale

    def start_back(which):
        from_modes(which, (mlp_forward, mlp_backward)[which]())

    def step_in(at):
        which, chunk = divmod(at, chunks)
        drained("x", which, chunk)
        if at == chunks - 1:
            send_pack()
        if at + 1 < 2 * chunks:
            send_rows(*divmod(at + 1, chunks))
        wave_in(which, chunk)
        spectra_out(which, chunk)

    steps = [
        (step_in, 0),
        (step_in, 1),
        (step_in, 2),
        (step_in, 3),
        (forward_pack,),
        (build_weights,),
        (into_modes, 0),
        (start_back, 0),
        (send_back, 0, 0),
        (step_in, 4),
        (step_in, 5),
        (drained, "back", 0, 0),
        (send_back, 0, 1),
        (back_rows, 0, 0),
        (wave_out, 0, 0),
        (drained, "back", 0, 1),
        (send_back, 0, 2),
        (back_rows, 0, 1),
        (wave_out, 0, 1),
        (into_modes, 1),
        (start_back, 1),
        (drained, "back", 0, 2),
        (send_back, 1, 0),
        (back_rows, 0, 2),
        (grad_partials,),
        (wave_out, 0, 2),
        (grad_chip,),
        (drained, "back", 1, 0),
        (send_back, 1, 1),
        (back_rows, 1, 0),
        (wave_out, 1, 0),
        (grad_over_y,),
        (drained, "back", 1, 1),
        (send_back, 1, 2),
        (back_rows, 1, 1),
        (grad_over_z,),
        (wave_out, 1, 1),
        (back_rows, 1, 2),
        (wave_out, 1, 2),
        (grad_back_z,),
        (grad_back_y,),
        (grad_finish,),
    ]
    for run, *at in steps:
        run(*at)

    for key in list(coming):
        received(*key)
    for key in list(leaving):
        drained(*key)


def per_device(fields, cotangent, kept_mask, w_one, b_one, w_two, b_two):
    lat_count = lax.axis_size("lat")
    lon_count = lax.axis_size("lon")
    samples, _, local_w, channels = fields.shape
    lon_cells = local_w * lon_count
    block = w_one.shape[2]
    span = channels // 2
    width = span // CHUNKS
    kept = 4 * lat_count
    rows = 16 * lat_count
    tables = ordered_tables(lat_count, lon_cells)
    share = -(-(4 * block + AUX) // (16 * lat_count)) * 16
    grad_rows = share * lat_count
    lat_y = min(4, lat_count)
    lat_z = lat_count // lat_y

    vmem = pl.BlockSpec(memory_space=pltpu.VMEM)
    anywhere = pl.BlockSpec(memory_space=pl.ANY)
    hbm = pl.BlockSpec(memory_space=pltpu.HBM)
    dma = pltpu.SemaphoreType.DMA
    scratch = [
        [pltpu.VMEM(table.shape, BF16) for table in tables],
        pltpu.VMEM((2, 2, block, block), BF16),
        pltpu.VMEM((2, 2, block), BF16),
        pltpu.VMEM((4, kept), jnp.int32),
        pltpu.VMEM((AUX, 128), F32),
        pltpu.VMEM((2, CHUNKS, 4, lon_cells, width), BF16),
        pltpu.VMEM((2, CHUNKS, rows, 2 * width), BF16),
        pltpu.VMEM((2, CHUNKS, rows // 2, 2 * width), BF16),
        pltpu.VMEM((2, CHUNKS, rows, 2 * width), BF16),
        pltpu.VMEM((2, CHUNKS, rows, 2 * width), BF16),
        pltpu.VMEM((2, 2 * kept, 2 * span), BF16),
        pltpu.VMEM((2, 2 * kept, 2 * span), BF16),
        pltpu.VMEM((2, CHUNKS, rows, 2 * width), BF16),
        pltpu.VMEM((2, CHUNKS, rows, 2 * width), BF16),
        pltpu.VMEM((2, CHUNKS, rows // 2, 2 * width), BF16),
        pltpu.VMEM((2, CHUNKS, 2, rows // 2, 2 * width), BF16),
        pltpu.VMEM((2, CHUNKS, 4, lon_cells, width), BF16),
        pltpu.VMEM((4 * block + AUX, 128), BF16),
        pltpu.VMEM((4, 4 * block + AUX, 128), BF16),
        pltpu.VMEM((4, 128, span), BF16),
        pltpu.VMEM((rows, rows), BF16),
        pltpu.VMEM((rows, rows), BF16),
        pltpu.VMEM((2 * span, 2 * span), BF16),
        pltpu.VMEM((2 * span, 2 * span), BF16),
        pltpu.VMEM((8, 2 * span), F32),
        pltpu.VMEM((2 * kept, 2 * span), F32),
        pltpu.VMEM((2 * kept, 2 * span), BF16),
        pltpu.VMEM((2 * kept, 2 * span), F32),
        pltpu.VMEM((2 * kept, 2 * span), BF16),
        pltpu.VMEM((2, 2, grad_rows, 128), BF16),
        pltpu.VMEM((2, grad_rows, 128), BF16),
        pltpu.VMEM((2, grad_rows, 128), BF16),
        pltpu.VMEM((grad_rows, 128), BF16),
        pltpu.VMEM((grad_rows, 128), BF16),
        pltpu.VMEM((lat_y, share * lat_z, 128), BF16),
        pltpu.VMEM((share * lat_z, 128), BF16),
        pltpu.VMEM((lat_z, share, 128), BF16),
        pltpu.VMEM((share, 128), BF16),
        pltpu.VMEM((lat_z, share, 128), BF16),
        pltpu.VMEM((lat_y, lat_z, share, 128), BF16),
        dma((5 + len(tables),)),
        dma((2, CHUNKS)),
        dma((2, CHUNKS)),
        dma((2, CHUNKS)),
        dma((2, CHUNKS)),
        dma((2, CHUNKS)),
        dma((2, CHUNKS)),
        dma((2, CHUNKS)),
        dma((2, CHUNKS)),
        dma((2, CHUNKS)),
        dma((2, CHUNKS)),
        dma((2, CHUNKS)),
        dma((2, CHUNKS)),
        dma((3,)),
        dma((4,)),
        dma((6,)),
        dma((6,)),
    ]
    scale = 1.0 / math.sqrt(samples * kept * kept)
    moved = 4 * samples * fields.shape[1] * local_w * channels * 2
    wave_y, wave_g, grads = pl.pallas_call(
        functools.partial(kernel, lat_count, block, scale),
        out_shape=(
            jax.ShapeDtypeStruct(fields.shape, BF16),
            jax.ShapeDtypeStruct(fields.shape, BF16),
            jax.ShapeDtypeStruct((grad_rows, 128), F32),
        ),
        in_specs=[hbm] * 7 + [[hbm] * len(tables)],
        out_specs=(anywhere, anywhere, vmem),
        scratch_shapes=scratch,
        compiler_params=pltpu.CompilerParams(
            collective_id=0, has_side_effects=True, vmem_limit_bytes=60 * 1024 * 1024
        ),
        cost_estimate=pl.CostEstimate(
            flops=6 * 10**9, bytes_accessed=moved, transcendentals=4 * kept * span
        ),
    )(
        fields,
        cotangent,
        w_one[0],
        w_two[0],
        b_one[0],
        b_two[0],
        kept_mask[:, :, 0].T,
        [jnp.asarray(table) for table in tables],
    )
    mixed = (fields.astype(F32) + wave_y.astype(F32)).astype(BF16)
    grad_fields = (cotangent.astype(F32) + wave_g.astype(F32)).astype(BF16)
    tail = grads[4 * block : 4 * block + 4, :block]
    return (
        mixed,
        grad_fields,
        grads[: 2 * block, :block].reshape(1, 2, block, block),
        tail[:2].reshape(1, 2, block),
        grads[2 * block : 4 * block, :block].reshape(1, 2, block, block),
        tail[2:].reshape(1, 2, block),
    )


def solution(mesh):
    placed = (
        P(None, "lat", "lon", None),
        P(None, "lat", "lon", None),
        P(None, "lat", "lon"),
        P("lon", None, None, None),
        P("lon", None, None),
        P("lon", None, None, None),
        P("lon", None, None),
    )
    return jax.shard_map(
        per_device,
        mesh=mesh,
        in_specs=placed,
        out_specs=(
            P(None, "lat", "lon", None),
            P(None, "lat", "lon", None),
            P("lon", None, None, None),
            P("lon", None, None),
            P("lon", None, None, None),
            P("lon", None, None),
        ),
        check_vma=False,
    )
```

```python
import functools
import math

import jax
import jax.numpy as jnp
import numpy as np
from jax import lax
from jax.experimental import pallas as pl
from jax.experimental.pallas import tpu as pltpu
from jax.sharding import PartitionSpec as P

MESH = pl.DeviceIdType.MESH
BF16 = jnp.bfloat16
F32 = jnp.float32
CHUNKS = 3
AUX = 16


def wave_tables(lon_cells, kept_w):
    wavenumber = np.arange(kept_w, dtype=np.int32)
    position = np.arange(lon_cells, dtype=np.int32)
    angles = (wavenumber[:, None] * position[None, :] % lon_cells).astype(np.float32) * np.float32(
        2.0 * math.pi / lon_cells
    )
    factor = np.float32(1.0 / math.sqrt(lon_cells))
    forward = np.stack([np.cos(angles) * factor, -np.sin(angles) * factor], 0)
    weights = np.where(wavenumber == 0, 1.0, 2.0).astype(np.float32)
    inverse = forward * weights[None, :, None]
    return (forward.astype(BF16), inverse.astype(BF16))


def lat_tables(lat_cells, kept_h):
    wavenumber = np.arange(kept_h, dtype=np.int32)
    wavenumber = np.where(wavenumber < kept_h // 2, wavenumber, wavenumber - kept_h)
    position = np.arange(lat_cells, dtype=np.int32)
    angles = (wavenumber[:, None] * position[None, :] % lat_cells).astype(np.float32) * np.float32(
        2.0 * math.pi / lat_cells
    )
    factor = np.float32(1.0 / math.sqrt(lat_cells))
    cosine = np.cos(angles) * factor
    sine = np.sin(angles) * factor
    forward = np.stack([np.stack([cosine, sine], 1), np.stack([-sine, cosine], 1)], 0)
    return forward.astype(BF16)


def ordered_tables(lat_count, lon_cells):
    kept_w = 4 * lat_count
    lat_cells = 8 * lat_count
    forward, inverse = wave_tables(lon_cells, kept_w)

    def rows(table):
        shaped = table.reshape(2, lat_count, 2, 2, lon_cells)
        return np.ascontiguousarray(shaped.transpose(2, 3, 1, 0, 4).reshape(8 * lat_count, lon_cells))

    forward, inverse = rows(forward), rows(inverse)
    lat = lat_tables(lat_cells, lat_cells // 2)
    lat = np.ascontiguousarray(lat.transpose(0, 1, 3, 2).reshape(lat_cells, 2 * lat_cells))
    return (
        forward,
        inverse,
        np.ascontiguousarray(forward.T),
        np.ascontiguousarray(inverse.T),
        lat,
        np.ascontiguousarray(lat.T),
    )


def dot(left, right):
    return jnp.dot(left, right, preferred_element_type=F32)


def dot_nt(left, right):
    return lax.dot_general(left, right, (((1,), (1,)), ((), ())), preferred_element_type=F32)


def dot_tn(left, right):
    return lax.dot_general(left, right, (((0,), (0,)), ((), ())), preferred_element_type=F32)


def arrived(ref, sem):
    pltpu.make_async_copy(ref, ref, sem).wait()


def kernel(
    lat_count,
    block,
    scale,
    fields,
    cotangent,
    w_one,
    w_two,
    b_one,
    b_two,
    kept_in,
    tables_in,
    wave_y,
    wave_g,
    grads,
    tables,
    weights,
    biases,
    kept_blocks,
    extra_rows,
    rows_in,
    own_spec,
    sib_spec,
    lat_out,
    lat_in,
    modes,
    back_modes,
    back_out,
    back_in,
    sib_back,
    wave_spec,
    wave_rows,
    pack,
    packs,
    place,
    perm_out,
    perm_in,
    first,
    second,
    bias,
    mask,
    hidden,
    slope,
    grad_pre,
    grad_send,
    grad_core,
    grad_pair,
    grad_chip_in,
    grad_sum,
    grad_y,
    grad_y_sum,
    grad_z,
    grad_own,
    grad_z_all,
    grad_all,
    table_sem,
    x_send,
    x_recv,
    sib_send,
    sib_recv,
    lat_send,
    lat_recv,
    back_send,
    back_recv,
    sib_back_send,
    sib_back_recv,
    y_send,
    y_recv,
    pack_send,
    pack_recv,
    grad_send_sem,
    grad_recv_sem,
):
    n_lat = lat_count
    lat = lax.axis_index("lat")
    lon = lax.axis_index("lon")
    core = lax.rem(lon, 2)
    sibling = lon + 1 - 2 * core
    chip = lax.div(lon, 2)
    sample = lax.rem(chip, 2)
    half = lax.div(chip, 2)
    spec_rows = 2 * n_lat
    core_rows = 8 * n_lat
    kept = 4 * n_lat
    width = rows_in.shape[-1]
    chunks = rows_in.shape[1]
    span = chunks * width
    local_w = fields.shape[2]
    group = lax.rem(lon, 4)
    group_base = lon - group

    def lon_peer(i):
        return lax.rem(lon + i, 8)

    def lat_peer(i):
        return lax.rem(lat + i, n_lat)

    def remote(src, dst, send_sem, recv_sem, lat_to, lon_to):
        return pltpu.make_async_remote_copy(
            src_ref=src,
            dst_ref=dst,
            send_sem=send_sem,
            recv_sem=recv_sem,
            device_id=(lat_to, lon_to),
            device_id_type=MESH,
        )

    barrier = pltpu.get_barrier_semaphore()

    def greet_lon(i, carry):
        pl.semaphore_signal(barrier, inc=1, device_id=(lat, lon_peer(i)), device_id_type=MESH)
        return carry

    def greet_lat(i, carry):
        pl.semaphore_signal(barrier, inc=1, device_id=(lat_peer(i), lon), device_id_type=MESH)
        return carry

    lax.fori_loop(1, 8, greet_lon, 0)
    lax.fori_loop(1, n_lat, greet_lat, 0)
    small = (
        (w_one, weights.at[0]),
        (w_two, weights.at[1]),
        (b_one, biases.at[0]),
        (b_two, biases.at[1]),
        (kept_in, kept_blocks),
    )
    loads = [
        pltpu.make_async_copy(source, target, table_sem.at[at])
        for at, (source, target) in enumerate(small + tuple(zip(tables_in, tables)))
    ]
    for load in loads:
        load.start()
    total_rows = 16 * n_lat
    out_row = lax.broadcasted_iota(jnp.int32, (total_rows, total_rows), 0)
    in_row = lax.broadcasted_iota(jnp.int32, (total_rows, total_rows), 1)

    def spread(row):
        return ((row >> 1) & 7) * spec_rows + (row >> 4) * 2 + (row & 1)

    perm_out[...] = (spread(out_row) == in_row).astype(F32).astype(BF16)
    perm_in[...] = (spread(in_row) == out_row).astype(F32).astype(BF16)
    lane_in = lax.broadcasted_iota(jnp.int32, (128, span), 0)
    lane_out = lax.broadcasted_iota(jnp.int32, (128, span), 1)
    for n in range(4):
        place[n] = (
            jnp.where(lane_in < block, lane_in + n * block, -1) == lane_out
        ).astype(F32).astype(BF16)

    for load in loads[: len(small)]:
        load.wait()
    pack[...] = jnp.zeros_like(pack)
    for at in range(2):
        pack[at * block : (at + 1) * block, :block] = weights[0, at]
        pack[(2 + at) * block : (3 + at) * block, :block] = weights[1, at]
    extra_rows[...] = jnp.zeros_like(extra_rows)
    extra_rows[0:2, :block] = biases[0].astype(F32)
    extra_rows[2:4, :block] = biases[1].astype(F32)
    extra_rows[4:8, :kept] = kept_blocks[...].astype(F32)
    pack[4 * block :, :] = extra_rows[...].astype(BF16)

    pl.semaphore_wait(barrier, 7 + n_lat - 1)

    leaving = {}
    coming = {}

    def drained(*key):
        if key in leaving:
            arrived(*leaving.pop(key))

    def received(*key):
        if key in coming:
            arrived(*coming.pop(key))

    def x_block(source, owner, chunk):
        owner_core = lax.rem(owner, 2)
        owner_chip = lax.div(owner, 2)
        lanes = pl.multiple_of(lax.div(owner_chip, 2) * span + chunk * width, 128)
        return source.at[
            lax.rem(owner_chip, 2), pl.ds(owner_core * 4, 4), :, pl.ds(lanes, width)
        ]

    def x_slot(which, chunk):
        here = pl.multiple_of(lon * local_w, local_w)
        return rows_in.at[which, chunk, :, pl.ds(here, local_w), :]

    def send_rows(which, chunk):
        source = (fields, cotangent)[which]

        def step(i, carry):
            to = lon_peer(i)
            remote(
                x_block(source, to, chunk),
                x_slot(which, chunk),
                x_send.at[which, chunk],
                x_recv.at[which, chunk],
                lat,
                to,
            ).start()
            return carry

        lax.fori_loop(1, 8, step, 0)
        pltpu.make_async_copy(
            x_block(source, lon, chunk), x_slot(which, chunk), x_recv.at[which, chunk]
        ).start()
        leaving["x", which, chunk] = (
            rows_in.at[which, chunk, :, : 7 * local_w, :],
            x_send.at[which, chunk],
        )
        coming["x", which, chunk] = (rows_in.at[which, chunk], x_recv.at[which, chunk])

    send_rows(0, 0)

    partner = lon + 2 - 4 * sample
    partner_slot = group + 2 - 4 * sample

    def send_pack():
        for at, to in enumerate((partner, sibling)):
            remote(pack, packs.at[group], pack_send.at[at], pack_recv.at[at], lat, to).start()
            leaving["pack", at] = (pack, pack_send.at[at])
            coming["pack", at] = (pack, pack_recv.at[at])
        pltpu.make_async_copy(pack, packs.at[group], pack_recv.at[3]).start()
        coming["pack", 3] = (pack, pack_recv.at[3])

    def forward_pack():
        received("pack", 0)
        theirs = packs.at[partner_slot]
        remote(theirs, theirs, pack_send.at[2], pack_recv.at[2], lat, sibling).start()
        leaving["pack", 2] = (pack, pack_send.at[2])
        coming["pack", 2] = (pack, pack_recv.at[2])

    for load in loads[len(small) :]:
        load.wait()
    wave_fwd, wave_inv, wave_fwd_t, wave_inv_t, lat_fwd, lat_inv = tables

    def wave_in(which, chunk):
        matrix = (wave_fwd, wave_inv)[which]
        received("x", which, chunk)

        def step(hh, carry):
            block_rows = rows_in[which, chunk, hh]
            own_rows = pl.multiple_of(core * kept, kept)
            sib_rows = pl.multiple_of((1 - core) * kept, kept)
            own = dot(matrix[pl.ds(own_rows, kept), :], block_rows).astype(BF16)
            sib = dot(matrix[pl.ds(sib_rows, kept), :], block_rows).astype(BF16)
            own_at = pl.multiple_of(core * core_rows + hh * spec_rows, spec_rows)
            sib_at = pl.multiple_of(hh * spec_rows, spec_rows)
            for k2 in range(2):
                lanes = slice(k2 * width, (k2 + 1) * width)
                piece = slice(k2 * spec_rows, (k2 + 1) * spec_rows)
                own_spec[which, chunk, pl.ds(own_at, spec_rows), lanes] = own[piece]
                sib_spec[which, chunk, pl.ds(sib_at, spec_rows), lanes] = sib[piece]
            return carry

        lax.fori_loop(0, 4, step, 0)
        there = pl.multiple_of(core * core_rows, core_rows)
        remote(
            sib_spec.at[which, chunk],
            own_spec.at[which, chunk, pl.ds(there, core_rows), :],
            sib_send.at[which, chunk],
            sib_recv.at[which, chunk],
            lat,
            sibling,
        ).start()
        leaving["sib", which, chunk] = (sib_spec.at[which, chunk], sib_send.at[which, chunk])
        coming["sib", which, chunk] = (sib_spec.at[which, chunk], sib_recv.at[which, chunk])

    def send_lat(name, source, target, send_sem, recv_sem, which, chunk):
        def rows_of(ref, at):
            return ref.at[which, chunk, pl.ds(pl.multiple_of(at * 16, 16), 16), :]

        def step(i, carry):
            to = lat_peer(i)
            remote(
                rows_of(source, to),
                rows_of(target, lat),
                send_sem.at[which, chunk],
                recv_sem.at[which, chunk],
                to,
                lon,
            ).start()
            return carry

        lax.fori_loop(1, n_lat, step, 0)
        pltpu.make_async_copy(
            rows_of(source, lat), rows_of(target, lat), recv_sem.at[which, chunk]
        ).start()
        leaving[name, which, chunk] = (
            source.at[which, chunk, : 16 * (n_lat - 1), :],
            send_sem.at[which, chunk],
        )
        coming[name, which, chunk] = (target.at[which, chunk], recv_sem.at[which, chunk])

    def spectra_out(which, chunk):
        received("sib", which, chunk)
        lat_out[which, chunk] = dot(perm_out[...], own_spec[which, chunk]).astype(BF16)
        send_lat("lat", lat_out, lat_in, lat_send, lat_recv, which, chunk)

    def into_modes(which):
        for chunk in range(chunks):
            received("lat", which, chunk)
            result = dot(lat_fwd[...], lat_in[which, chunk]).astype(BF16)
            for q in range(2):
                for k2 in range(2):
                    modes[
                        which,
                        k2 * kept : (k2 + 1) * kept,
                        q * span + chunk * width : q * span + (chunk + 1) * width,
                    ] = result[q * kept : (q + 1) * kept, k2 * width : (k2 + 1) * width]

    def from_modes(which, values):
        back_modes[which] = values
        for chunk in range(chunks):
            rows = []
            for q in range(2):
                lanes = slice(q * span + chunk * width, q * span + (chunk + 1) * width)
                rows.append(
                    jnp.concatenate(
                        [back_modes[which, :kept, lanes], back_modes[which, kept:, lanes]], 1
                    )
                )
            spectrum = jnp.concatenate(rows, 0)
            back_out[which, chunk] = dot(lat_inv[...], spectrum).astype(BF16)

    def send_back(which, chunk):
        send_lat("back", back_out, back_in, back_send, back_recv, which, chunk)

    def back_rows(which, chunk):
        received("back", which, chunk)
        own_rows = pl.multiple_of(core * core_rows, core_rows)
        sib_rows = pl.multiple_of((1 - core) * core_rows, core_rows)
        landed = back_in[which, chunk]
        sib_back[which, chunk] = dot(perm_in[pl.ds(sib_rows, core_rows), :], landed).astype(BF16)
        remote(
            sib_back.at[which, chunk],
            wave_spec.at[which, chunk, core],
            sib_back_send.at[which, chunk],
            sib_back_recv.at[which, chunk],
            lat,
            sibling,
        ).start()
        block_of = sib_back.at[which, chunk]
        leaving["sib_back", which, chunk] = (block_of, sib_back_send.at[which, chunk])
        coming["sib_back", which, chunk] = (block_of, sib_back_recv.at[which, chunk])
        wave_spec[which, chunk, core] = dot(
            perm_in[pl.ds(own_rows, core_rows), :], landed
        ).astype(BF16)

    def wave_out(which, chunk):
        matrix = (wave_inv_t, wave_fwd_t)[which]
        target = (wave_y, wave_g)[which]
        received("sib_back", which, chunk)

        def step(hh, carry):
            at = pl.ds(pl.multiple_of(hh * spec_rows, spec_rows), spec_rows)
            spectrum = jnp.concatenate(
                [
                    wave_spec[which, chunk, side, at, k2 * width : (k2 + 1) * width]
                    for side in range(2)
                    for k2 in range(2)
                ],
                0,
            )
            wave_rows[which, chunk, hh] = dot(matrix[...], spectrum).astype(BF16)
            return carry

        lax.fori_loop(0, 4, step, 0)
        lanes = pl.multiple_of(half * span + chunk * width, 128)
        slot = target.at[sample, pl.ds(core * 4, 4), :, pl.ds(lanes, width)]

        def columns(to):
            return wave_rows.at[
                which, chunk, :, pl.ds(pl.multiple_of(to * local_w, local_w), local_w), :
            ]

        def send(i, carry):
            to = lon_peer(i)
            remote(
                columns(to), slot, y_send.at[which, chunk], y_recv.at[which, chunk], lat, to
            ).start()
            return carry

        lax.fori_loop(1, 8, send, 0)
        pltpu.make_async_copy(columns(lon), slot, y_recv.at[which, chunk]).start()
        leaving["y", which, chunk] = (
            wave_rows.at[which, chunk, :, : 7 * local_w, :],
            y_send.at[which, chunk],
        )
        coming["y", which, chunk] = (
            target.at[:, :, :, : 2 * width],
            y_recv.at[which, chunk],
        )

    def build_weights():
        for at in range(1, 4):
            received("pack", at)
        for n in range(4):
            rows = slice(n * block, (n + 1) * block)
            below = slice(span + n * block, span + (n + 1) * block)
            for at, target in ((0, first), (2, second)):
                real = dot(packs[n, at * block : (at + 1) * block, :], place[n])
                imag = dot(packs[n, (at + 1) * block : (at + 2) * block, :], place[n])
                target[rows, :span] = real.astype(BF16)
                target[rows, span:] = imag.astype(BF16)
                target[below, :span] = (-imag).astype(BF16)
                target[below, span:] = real.astype(BF16)
        extra = [packs[n, 4 * block :, :] for n in range(4)]
        spread_bias = sum(dot(extra[n], place[n]) for n in range(4))
        bias[0:1, :span] = spread_bias[0:1]
        bias[0:1, span:] = spread_bias[1:2]
        bias[1:2, :span] = spread_bias[2:3]
        bias[1:2, span:] = spread_bias[3:4]
        stacked = jnp.concatenate(extra, 0)
        row = lax.broadcasted_iota(jnp.int32, (4 * AUX, span), 0)
        lane = lax.broadcasted_iota(jnp.int32, (4 * AUX, span), 1)
        low = (row >> 4) * block
        inside = (lane >= low) & (lane < low + block)
        for k2 in range(2):
            chosen = inside & ((row & (AUX - 1)) == 4 + 2 * core + k2)
            kept_here = dot_tn(stacked, chosen.astype(F32).astype(BF16))[:kept]
            mask[k2 * kept : (k2 + 1) * kept, :span] = kept_here
            mask[k2 * kept : (k2 + 1) * kept, span:] = kept_here

    def mlp_forward():
        pre = dot(modes[0], first[...]) + bias[0:1, :]
        cumulative = 0.5 * (1.0 + lax.erf(pre * (1.0 / math.sqrt(2.0))))
        density = jnp.exp(-0.5 * pre * pre) * (1.0 / math.sqrt(2.0 * math.pi))
        hidden[...] = (pre * cumulative).astype(BF16)
        slope[...] = cumulative + pre * density
        output = dot(hidden[...], second[...]) + bias[1:2, :]
        return (mask[...] * output).astype(BF16)

    def mlp_backward():
        modes[1] = (mask[...] * modes[1].astype(F32)).astype(BF16)
        grad_hidden = dot_nt(modes[1], second[...])
        grad_pre[...] = (grad_hidden * slope[...]).astype(BF16)
        return dot_nt(grad_pre[...], first[...]).astype(BF16)

    def grad_partials():
        sums = []
        for at, (left, right) in enumerate(((modes.at[0], grad_pre), (hidden, modes.at[1]))):
            total = dot_tn(left[...], right[...])
            parts = (
                total[:span, :span] + total[span:, span:],
                total[:span, span:] - total[span:, :span],
            )
            for which, part in enumerate(parts):
                part = part.astype(BF16)
                for n in range(4):
                    grad_send[
                        n % 2, n // 2, (2 * at + which) * block : (2 * at + which + 1) * block, :
                    ] = dot_nt(part[n * block : (n + 1) * block, :], place[n]).astype(BF16)
            summed = jnp.sum(right[...].astype(F32), 0, keepdims=True)
            sums += [summed[:, :span], summed[:, span:]]
        row = lax.broadcasted_iota(jnp.int32, (AUX, span), 0)
        stacked = jnp.zeros((AUX, span), F32)
        for at, value in enumerate(sums):
            stacked = jnp.where(row == at, value, stacked)
        stacked = stacked.astype(BF16)
        tail = grad_send.shape[2] - 4 * block - AUX
        for n in range(4):
            grad_send[n % 2, n // 2, 4 * block : 4 * block + AUX, :] = dot_nt(
                stacked, place[n]
            ).astype(BF16)
            if tail:
                grad_send[n % 2, n // 2, 4 * block + AUX :, :] = jnp.zeros((tail, 128), BF16)

        grad_copy("core", grad_send.at[1 - core], grad_core, 0, lat, sibling)

    def grad_copy(key, source, target, at, lat_to, lon_to):
        remote(source, target, grad_send_sem.at[at], grad_recv_sem.at[at], lat_to, lon_to).start()
        leaving[key,] = (source, grad_send_sem.at[at])
        coming[key,] = (target, grad_recv_sem.at[at])

    def grad_exchange(key, source_of, target, slot, count, at, to_lat):
        def step(i, carry):
            to = lax.rem(slot + i, count)
            remote(
                source_of(to),
                target.at[slot],
                grad_send_sem.at[at],
                grad_recv_sem.at[at],
                to_lat(to),
                lon,
            ).start()
            return carry

        lax.fori_loop(1, count, step, 0)
        pltpu.make_async_copy(source_of(slot), target.at[slot], grad_recv_sem.at[at]).start()
        leaving[key,] = (target.at[: count - 1], grad_send_sem.at[at])
        coming[key,] = (target, grad_recv_sem.at[at])

    n_z, n_y = grad_z.shape[0], grad_y.shape[0]
    z, y = lax.div(lat, n_y), lax.rem(lat, n_y)
    z_share, y_share = grad_z.shape[1], grad_y.shape[1]

    def along_z(to):
        return to * n_y + y

    def along_y(to):
        return z * n_y + to

    def grad_chip():
        received("core")
        grad_pair[...] = (grad_send[core].astype(F32) + grad_core[...].astype(F32)).astype(BF16)
        grad_copy("chip", grad_pair.at[1 - sample], grad_chip_in, 1, lat, partner)

    def grad_over_y():
        received("chip")
        grad_sum[...] = (grad_pair[sample].astype(F32) + grad_chip_in[...].astype(F32)).astype(BF16)

        def part(to):
            return grad_sum.at[pl.ds(pl.multiple_of(to * y_share, 16), y_share), :]

        grad_exchange("y_sum", part, grad_y, y, n_y, 2, along_y)

    def grad_over_z():
        received("y_sum")
        grad_y_sum[...] = jnp.sum(grad_y[...].astype(F32), 0).astype(BF16)

        def part(to):
            return grad_y_sum.at[pl.ds(pl.multiple_of(to * z_share, 16), z_share), :]

        grad_exchange("z_sum", part, grad_z, z, n_z, 3, along_z)

    def grad_back_z():
        received("z_sum")
        grad_own[...] = jnp.sum(grad_z[...].astype(F32), 0).astype(BF16)
        grad_exchange("z_all", lambda to: grad_own, grad_z_all, z, n_z, 4, along_z)

    def grad_back_y():
        received("z_all")
        grad_exchange("y_all", lambda to: grad_z_all, grad_all, y, n_y, 5, along_y)

    def grad_finish():
        received("y_all")
        for part in range(n_y):
            for piece in range(n_z):
                low = part * y_share + piece * z_share
                grads[low : low + z_share, :] = grad_all[part, piece].astype(F32) * scale

    def start_back(which):
        from_modes(which, (mlp_forward, mlp_backward)[which]())

    def step_in(at):
        which, chunk = divmod(at, chunks)
        drained("x", which, chunk)
        if at + 1 < 2 * chunks:
            send_rows(*divmod(at + 1, chunks))
        if at == chunks - 1:
            send_pack()
        wave_in(which, chunk)
        spectra_out(which, chunk)

    steps = [
        (step_in, 0),
        (step_in, 1),
        (step_in, 2),
        (step_in, 3),
        (forward_pack,),
        (build_weights,),
        (into_modes, 0),
        (start_back, 0),
        (send_back, 0, 0),
        (step_in, 4),
        (step_in, 5),
        (drained, "back", 0, 0),
        (send_back, 0, 1),
        (back_rows, 0, 0),
        (wave_out, 0, 0),
        (drained, "back", 0, 1),
        (send_back, 0, 2),
        (back_rows, 0, 1),
        (wave_out, 0, 1),
        (into_modes, 1),
        (start_back, 1),
        (drained, "back", 0, 2),
        (send_back, 1, 0),
        (back_rows, 0, 2),
        (grad_partials,),
        (wave_out, 0, 2),
        (grad_chip,),
        (drained, "back", 1, 0),
        (send_back, 1, 1),
        (back_rows, 1, 0),
        (wave_out, 1, 0),
        (grad_over_y,),
        (drained, "back", 1, 1),
        (send_back, 1, 2),
        (back_rows, 1, 1),
        (grad_over_z,),
        (wave_out, 1, 1),
        (back_rows, 1, 2),
        (wave_out, 1, 2),
        (grad_back_z,),
        (grad_back_y,),
        (grad_finish,),
    ]
    for run, *at in steps:
        run(*at)

    for key in list(coming):
        received(*key)
    for key in list(leaving):
        drained(*key)


def per_device(fields, cotangent, kept_mask, w_one, b_one, w_two, b_two):
    lat_count = lax.axis_size("lat")
    lon_count = lax.axis_size("lon")
    samples, _, local_w, channels = fields.shape
    lon_cells = local_w * lon_count
    block = w_one.shape[2]
    span = channels // 2
    width = span // CHUNKS
    kept = 4 * lat_count
    rows = 16 * lat_count
    tables = ordered_tables(lat_count, lon_cells)
    share = -(-(4 * block + AUX) // (16 * lat_count)) * 16
    grad_rows = share * lat_count
    lat_y = min(4, lat_count)
    lat_z = lat_count // lat_y

    vmem = pl.BlockSpec(memory_space=pltpu.VMEM)
    anywhere = pl.BlockSpec(memory_space=pl.ANY)
    hbm = pl.BlockSpec(memory_space=pltpu.HBM)
    dma = pltpu.SemaphoreType.DMA
    scratch = [
        [pltpu.VMEM(table.shape, BF16) for table in tables],
        pltpu.VMEM((2, 2, block, block), BF16),
        pltpu.VMEM((2, 2, block), BF16),
        pltpu.VMEM((4, kept), jnp.int32),
        pltpu.VMEM((AUX, 128), F32),
        pltpu.VMEM((2, CHUNKS, 4, lon_cells, width), BF16),
        pltpu.VMEM((2, CHUNKS, rows, 2 * width), BF16),
        pltpu.VMEM((2, CHUNKS, rows // 2, 2 * width), BF16),
        pltpu.VMEM((2, CHUNKS, rows, 2 * width), BF16),
        pltpu.VMEM((2, CHUNKS, rows, 2 * width), BF16),
        pltpu.VMEM((2, 2 * kept, 2 * span), BF16),
        pltpu.VMEM((2, 2 * kept, 2 * span), BF16),
        pltpu.VMEM((2, CHUNKS, rows, 2 * width), BF16),
        pltpu.VMEM((2, CHUNKS, rows, 2 * width), BF16),
        pltpu.VMEM((2, CHUNKS, rows // 2, 2 * width), BF16),
        pltpu.VMEM((2, CHUNKS, 2, rows // 2, 2 * width), BF16),
        pltpu.VMEM((2, CHUNKS, 4, lon_cells, width), BF16),
        pltpu.VMEM((4 * block + AUX, 128), BF16),
        pltpu.VMEM((4, 4 * block + AUX, 128), BF16),
        pltpu.VMEM((4, 128, span), BF16),
        pltpu.VMEM((rows, rows), BF16),
        pltpu.VMEM((rows, rows), BF16),
        pltpu.VMEM((2 * span, 2 * span), BF16),
        pltpu.VMEM((2 * span, 2 * span), BF16),
        pltpu.VMEM((8, 2 * span), F32),
        pltpu.VMEM((2 * kept, 2 * span), F32),
        pltpu.VMEM((2 * kept, 2 * span), BF16),
        pltpu.VMEM((2 * kept, 2 * span), F32),
        pltpu.VMEM((2 * kept, 2 * span), BF16),
        pltpu.VMEM((2, 2, grad_rows, 128), BF16),
        pltpu.VMEM((2, grad_rows, 128), BF16),
        pltpu.VMEM((2, grad_rows, 128), BF16),
        pltpu.VMEM((grad_rows, 128), BF16),
        pltpu.VMEM((grad_rows, 128), BF16),
        pltpu.VMEM((lat_y, share * lat_z, 128), BF16),
        pltpu.VMEM((share * lat_z, 128), BF16),
        pltpu.VMEM((lat_z, share, 128), BF16),
        pltpu.VMEM((share, 128), BF16),
        pltpu.VMEM((lat_z, share, 128), BF16),
        pltpu.VMEM((lat_y, lat_z, share, 128), BF16),
        dma((5 + len(tables),)),
        dma((2, CHUNKS)),
        dma((2, CHUNKS)),
        dma((2, CHUNKS)),
        dma((2, CHUNKS)),
        dma((2, CHUNKS)),
        dma((2, CHUNKS)),
        dma((2, CHUNKS)),
        dma((2, CHUNKS)),
        dma((2, CHUNKS)),
        dma((2, CHUNKS)),
        dma((2, CHUNKS)),
        dma((2, CHUNKS)),
        dma((3,)),
        dma((4,)),
        dma((6,)),
        dma((6,)),
    ]
    scale = 1.0 / math.sqrt(samples * kept * kept)
    moved = 4 * samples * fields.shape[1] * local_w * channels * 2
    wave_y, wave_g, grads = pl.pallas_call(
        functools.partial(kernel, lat_count, block, scale),
        out_shape=(
            jax.ShapeDtypeStruct(fields.shape, BF16),
            jax.ShapeDtypeStruct(fields.shape, BF16),
            jax.ShapeDtypeStruct((grad_rows, 128), F32),
        ),
        in_specs=[hbm] * 7 + [[hbm] * len(tables)],
        out_specs=(anywhere, anywhere, vmem),
        scratch_shapes=scratch,
        compiler_params=pltpu.CompilerParams(
            collective_id=0, has_side_effects=True, vmem_limit_bytes=60 * 1024 * 1024
        ),
        cost_estimate=pl.CostEstimate(
            flops=6 * 10**9, bytes_accessed=moved, transcendentals=4 * kept * span
        ),
    )(
        fields,
        cotangent,
        w_one[0],
        w_two[0],
        b_one[0],
        b_two[0],
        kept_mask[:, :, 0].T,
        [jnp.asarray(table) for table in tables],
    )
    mixed = (fields.astype(F32) + wave_y.astype(F32)).astype(BF16)
    grad_fields = (cotangent.astype(F32) + wave_g.astype(F32)).astype(BF16)
    tail = grads[4 * block : 4 * block + 4, :block]
    return (
        mixed,
        grad_fields,
        grads[: 2 * block, :block].reshape(1, 2, block, block),
        tail[:2].reshape(1, 2, block),
        grads[2 * block : 4 * block, :block].reshape(1, 2, block, block),
        tail[2:].reshape(1, 2, block),
    )


def solution(mesh):
    placed = (
        P(None, "lat", "lon", None),
        P(None, "lat", "lon", None),
        P(None, "lat", "lon"),
        P("lon", None, None, None),
        P("lon", None, None),
        P("lon", None, None, None),
        P("lon", None, None),
    )
    return jax.shard_map(
        per_device,
        mesh=mesh,
        in_specs=placed,
        out_specs=(
            P(None, "lat", "lon", None),
            P(None, "lat", "lon", None),
            P("lon", None, None, None),
            P("lon", None, None),
            P("lon", None, None, None),
            P("lon", None, None),
        ),
        check_vma=False,
    )
```
